256 devices in a mesh: pair: 2 (over y_hi), ctx: 8 (over x, core), batch: 16 (over z, y_lo).
Axes of the slice: x: 4, y: 4 (y_hi: 2, y_lo: 2; y = y_hi * 2 + y_lo), z: 8, core: 2. Of those that a mesh axis runs over, the one named last changes fastest.
Arguments:
- prompt_keys: bfloat16 [49152, 512], P(('batch', 'pair', 'ctx')), parts along dimension 0, may hold values from -5 to 5
- prompt_values: bfloat16 [49152, 512], P(('batch', 'pair', 'ctx')), parts along dimension 0, may hold values from -6 to 6
- resp_queries: bfloat16 [2, 16384, 2048], P('pair', ('batch', 'ctx')), parts along dimension 1, may hold values from -100 to 100
- resp_keys: bfloat16 [2, 16384, 512], P('pair', ('batch', 'ctx')), parts along dimension 1, may hold values from -6 to 6
- resp_values: bfloat16 [2, 16384, 512], P('pair', ('batch', 'ctx')), parts along dimension 1, may hold values from -6 to 6
- out_grad: bfloat16 [2, 16384, 2048], P('pair', ('batch', 'ctx')), parts along dimension 1, may hold values from -6 to 6
- lengths: int32 [32], P(('batch', 'pair')), parts along dimension 0, may hold values from 256 to 1024, as said below
Outputs:
- attn_out: bfloat16 [2, 16384, 2048], P('pair', ('batch', 'ctx')), parts along dimension 1
- query_grad: bfloat16 [2, 16384, 2048], P('pair', ('batch', 'ctx')), parts along dimension 1
- resp_key_grad: bfloat16 [2, 16384, 512], P('pair', ('batch', 'ctx')), parts along dimension 1
- resp_value_grad: bfloat16 [2, 16384, 512], P('pair', ('batch', 'ctx')), parts along dimension 1
- prompt_key_grad: bfloat16 [49152, 512], P(('batch', 'pair', 'ctx')), parts along dimension 0
- prompt_value_grad: bfloat16 [49152, 512], P(('batch', 'pair', 'ctx')), parts along dimension 0
The draws below stay inside these ranges and needn't reach their ends.
There are 16 independent parts, one for each index of `batch`. The reference program is written for one: setup_inputs(seed, part) draws one part's arguments, and reference() takes and returns one part's arrays. A program takes and returns all parts, laid end to end along the dimension named above; each array names one. Nothing has to cross between parts.
Inputs may be any that keep to these rules, and one draw needn't show every extreme that they name: One of the two lengths is exactly 1024.
All inputs are finite; a program needn't handle non-finite values.
Results may differ from the reference program's by a relative error of at most 0.028.
Values may be sent and summed in bfloat16 or wider, within the bound.
No kernel may reach another device: no remote copies, remote signals or barrier semaphores. Data moves between devices by JAX's collectives and lax.ppermute only.
A program may use at most 128 MiB of HBM per device.

```python
import jax
import jax.numpy as jnp
from jax import lax

HEADS = 16
KV_HEADS = 4
HEAD_DIM = 128
PROMPT = 3072
RESP = 1024


def prompt_key_base(key):
    base = jax.random.normal(jax.random.fold_in(key, 101), (PROMPT, KV_HEADS * HEAD_DIM), jnp.float32)
    return jnp.clip(base, -5.0, 5.0)


def draw_prompt_keys(key, part):
    return prompt_key_base(key).astype(jnp.bfloat16)


def draw_resp_queries(key, part):
    key = jax.random.fold_in(key, 7)
    shape_all = (2, RESP, HEADS * HEAD_DIM)
    result = jnp.clip(2.5 * jax.random.normal(jax.random.fold_in(key, 3), shape_all, jnp.float32), -15.0, 15.0)
    return result.astype(jnp.bfloat16)


def draw_lengths(key, part):
    key = jax.random.fold_in(key, 11)
    drawn = jax.random.randint(jax.random.fold_in(key, 1), (2,), RESP // 4, RESP + 1)
    which = jax.random.randint(jax.random.fold_in(key, 2), (), 0, 2)
    return jnp.where(jnp.arange(2) == which, RESP, drawn).astype(jnp.int32)


def level_of(own_key, extent, cuts, smallest, largest):
    factor_of = 1.0
    for position, blocks in cuts:
        heights = jax.random.uniform(jax.random.fold_in(jax.random.fold_in(own_key, 6), position), (blocks,), jnp.float32, smallest / len(cuts), largest / len(cuts))
        factor_of = factor_of * jnp.repeat(jnp.exp(heights), extent[position] // blocks).reshape((-1,) + (1,) * (len(extent) - 1 - position))
    return factor_of


def normal_values(own_key, shape, scale, bound, shards=(), kind=jnp.bfloat16):
    values = scale * jax.random.normal(own_key, shape, jnp.float32)
    if shards:
        values = values * level_of(own_key, shape, shards, -0.22, 0.18)
    return jnp.clip(values, -bound, bound).astype(kind)


def setup_inputs(seed: int = 0, part: int = 0) -> dict:
    arg_keys = jax.random.split(jax.random.key(seed), 8)
    own_keys = jax.random.split(jax.random.fold_in(arg_keys[7], part), 8)
    return {
        "prompt_keys": draw_prompt_keys(jax.random.fold_in(jax.random.fold_in(arg_keys[7], part), 71), part),
        "prompt_values": normal_values(own_keys[1], (PROMPT, KV_HEADS * HEAD_DIM), 1.0, 6.0, ((0, 16),)),
        "resp_queries": draw_resp_queries(jax.random.fold_in(jax.random.fold_in(arg_keys[7], part), 71), part),
        "resp_keys": normal_values(own_keys[3], (2, RESP, KV_HEADS * HEAD_DIM), 1.0, 6.0, ((0, 2), (1, 8))),
        "resp_values": normal_values(own_keys[4], (2, RESP, KV_HEADS * HEAD_DIM), 1.0, 6.0, ((0, 2), (1, 8))),
        "out_grad": normal_values(own_keys[5], (2, RESP, HEADS * HEAD_DIM), 1.0, 6.0, ((0, 2), (1, 8))),
        "lengths": draw_lengths(jax.random.fold_in(jax.random.fold_in(arg_keys[7], part), 71), part),
    }


def attend(queries, all_keys, all_values, cotangent, allowed, live_rows):
    row_count = queries.shape[0]
    key_count = all_keys.shape[0]
    group_size = HEADS // KV_HEADS
    score_scale = 1.0 / (HEAD_DIM ** 0.5)
    cot_live = jnp.where(live_rows[:, None], cotangent, jnp.zeros_like(cotangent))
    query_heads = jnp.transpose(queries.reshape(row_count, KV_HEADS, group_size, HEAD_DIM), (1, 0, 2, 3))
    grad_heads = jnp.transpose(cot_live.reshape(row_count, KV_HEADS, group_size, HEAD_DIM), (1, 0, 2, 3))
    key_heads = jnp.transpose(all_keys.reshape(key_count, KV_HEADS, HEAD_DIM), (1, 0, 2))
    value_heads = jnp.transpose(all_values.reshape(key_count, KV_HEADS, HEAD_DIM), (1, 0, 2))

    def per_head(packed):
        query_head, key_head, value_head, grad_head = packed
        query_wide = query_head.astype(jnp.float32)
        key_wide = key_head.astype(jnp.float32)
        value_wide = value_head.astype(jnp.float32)
        grad_wide = grad_head.astype(jnp.float32)
        scores = jnp.einsum("rgd,kd->rgk", query_wide, key_wide) * score_scale
        scores = jnp.where(allowed[:, None, :], scores, -jnp.inf)
        row_max = jnp.max(scores, axis=-1, keepdims=True)
        raised = jnp.exp(scores - row_max)
        row_sum = jnp.sum(raised, axis=-1, keepdims=True)
        weights = raised / row_sum
        weights_low = weights.astype(jnp.bfloat16)
        output = jnp.einsum("rgk,kd->rgd", weights_low.astype(jnp.float32), value_wide)
        output = jnp.where(live_rows[:, None, None], output, jnp.zeros_like(output))
        output_low = output.astype(jnp.bfloat16)
        row_dot = jnp.sum(grad_wide * output_low.astype(jnp.float32), axis=-1, keepdims=True)
        prob_grad = jnp.einsum("rgd,kd->rgk", grad_wide, value_wide)
        score_grad = (weights * (prob_grad - row_dot)).astype(jnp.bfloat16).astype(jnp.float32)
        dquery = jnp.einsum("rgk,kd->rgd", score_grad, key_wide) * score_scale
        key_grad = jnp.einsum("rgk,rgd->kd", score_grad, query_wide) * score_scale
        dvalue = jnp.einsum("rgk,rgd->kd", weights_low.astype(jnp.float32), grad_wide)
        return output_low, dquery, key_grad, dvalue

    stacked = lax.map(per_head, (query_heads, key_heads, value_heads, grad_heads))
    output = jnp.transpose(stacked[0], (1, 0, 2, 3)).reshape(row_count, HEADS * HEAD_DIM)
    dquery = jnp.transpose(stacked[1], (1, 0, 2, 3)).reshape(row_count, HEADS * HEAD_DIM)
    key_grad = jnp.transpose(stacked[2], (1, 0, 2)).reshape(key_count, KV_HEADS * HEAD_DIM)
    dvalue = jnp.transpose(stacked[3], (1, 0, 2)).reshape(key_count, KV_HEADS * HEAD_DIM)
    return output, dquery, key_grad, dvalue


def reference(prompt_keys, prompt_values, resp_queries, resp_keys, resp_values, out_grad, lengths):
    outputs = []
    qgrads = []
    kgrads = []
    vgrads = []
    for member in range(2):
        length = lengths[member]
        row_pos = jnp.arange(RESP, dtype=jnp.int32)
        key_pos = jnp.arange(PROMPT + RESP, dtype=jnp.int32) - PROMPT
        allowed = (key_pos[None, :] < 0) | ((key_pos[None, :] <= row_pos[:, None]) & (key_pos[None, :] < length))
        live_rows = row_pos < length
        all_keys = jnp.concatenate([prompt_keys, resp_keys[member]], axis=0)
        all_values = jnp.concatenate([prompt_values, resp_values[member]], axis=0)
        output, dquery, key_grad, dvalue = attend(resp_queries[member], all_keys, all_values, out_grad[member], allowed, live_rows)
        outputs.append(output)
        qgrads.append(dquery.astype(jnp.bfloat16))
        kgrads.append(key_grad)
        vgrads.append(dvalue)
    attn_out = jnp.stack(outputs)
    query_grad = jnp.stack(qgrads)
    resp_key_grad = jnp.stack([kgrads[0][PROMPT:], kgrads[1][PROMPT:]]).astype(jnp.bfloat16)
    resp_value_grad = jnp.stack([vgrads[0][PROMPT:], vgrads[1][PROMPT:]]).astype(jnp.bfloat16)
    prompt_key_grad = (kgrads[0][:PROMPT] + kgrads[1][:PROMPT]).astype(jnp.bfloat16)
    prompt_value_grad = (vgrads[0][:PROMPT] + vgrads[1][:PROMPT]).astype(jnp.bfloat16)
    return (attn_out, query_grad, resp_key_grad, resp_value_grad, prompt_key_grad, prompt_value_grad)
```

```python
import functools
import math

import jax
import jax.numpy as jnp
from jax import lax
from jax.experimental import pallas as pl
from jax.experimental.pallas import tpu as pltpu
from jax.sharding import PartitionSpec as P

F32 = jnp.float32
BF = jnp.bfloat16
SCALE = 1.0 / math.sqrt(128.0)
SCALE_LOG2 = math.log2(math.e) / math.sqrt(128.0)
CHIPS = 4
PROMPT_ROWS = 192
RESP_ROWS = 128
KEYS = 4096
PROMPT_KEYS = 3072
KEY_BLOCK = 768
VMEM = pl.BlockSpec(memory_space=pltpu.VMEM)
SMEM = pl.BlockSpec(memory_space=pltpu.SMEM)


def dot(a, b):
    return jnp.dot(a, b, preferred_element_type=F32)


def shape(dims, dtype=BF):
    return jax.ShapeDtypeStruct(dims, dtype)


def lanes(index, width):
    return pl.ds(pl.multiple_of(index * width, width), width)


def pack_keys(place, pk, pv, rk, rv, *outs):
    x = place[2]
    for d in range(CHIPS):
        head = lanes(lax.rem(x + d, CHIPS), 128)
        outs[d][0:PROMPT_ROWS, :] = pk[:, head]
        outs[d][PROMPT_ROWS:, :] = pv[:, head]
        outs[CHIPS + d][0:RESP_ROWS, :] = rk[:, head]
        outs[CHIPS + d][RESP_ROWS:, :] = rv[:, head]


def pack_rows(place, a, b, *outs):
    x = place[2]
    for d in range(CHIPS):
        heads = lanes(lax.rem(x + d, CHIPS), 512)
        outs[d][...] = a[:, heads]
        outs[CHIPS + d][...] = b[:, heads]


def unpack_rows(place, *refs):
    x = place[2]
    for which in range(2):
        for d in range(CHIPS):
            heads = lanes(lax.rem(x + d, CHIPS), 512)
            refs[2 * CHIPS + which][:, heads] = refs[which * CHIPS + d][...]


def unpack_keys(place, *refs):
    x = place[2]
    pk, pv, rk, rv = refs[2 * CHIPS :]
    for d in range(CHIPS):
        head = lanes(lax.rem(x + d, CHIPS), 128)
        pk[:, head] = refs[d][0:PROMPT_ROWS, :]
        pv[:, head] = refs[d][PROMPT_ROWS:, :]
        rk[:, head] = refs[CHIPS + d][0:RESP_ROWS, :]
        rv[:, head] = refs[CHIPS + d][RESP_ROWS:, :]


def sum_prompt(own, other, far, *outs):
    total = (own[...] + other[...].astype(F32) + far[...].astype(F32)).astype(BF)
    for d in range(CHIPS):
        outs[d][...] = total[2 * d * PROMPT_ROWS : 2 * (d + 1) * PROMPT_ROWS, :]


def sum_resp(own, other, *outs):
    total = (own[...] + other[...].astype(F32)).astype(BF)
    for d in range(CHIPS):
        outs[d][...] = total[2 * d * RESP_ROWS : 2 * (d + 1) * RESP_ROWS, :]


def attention(place, *refs):
    q_in, g_in = refs[0:4], refs[4:8]
    prompt_in = refs[8:12]
    resp_in = refs[12:14]
    o_out, dq_out = refs[14:18], refs[18:22]
    dprompt_out = refs[22:26]
    dresp_out = refs[26:28]
    (qs, gs, os_, qn, qT, gT, gn, kk, kT, vv, vT, sp, ee, ds_s, dq, dkp, dvp, dkr, dvr) = refs[28:]
    c, length, x = place[0], place[1], place[2]

    chip_of = [lax.rem(x + CHIPS - d, CHIPS) for d in range(CHIPS)]
    for d in range(CHIPS):
        qs[pl.ds(chip_of[d], 1)] = q_in[d][...][None]
        gs[pl.ds(chip_of[d], 1)] = g_in[d][...][None]
    for s in range(4):
        for d in range(CHIPS):
            at = slice(768 * s + PROMPT_ROWS * d, 768 * s + PROMPT_ROWS * (d + 1))
            off = 2 * PROMPT_ROWS * d
            kk[at, 0:128] = prompt_in[s][off : off + PROMPT_ROWS, :]
            vv[at, 0:128] = prompt_in[s][off + PROMPT_ROWS : off + 2 * PROMPT_ROWS, :]
    resp_at = []
    for s in range(2):
        for d in range(CHIPS):
            parity = c if s == 0 else 1 - c
            at = PROMPT_KEYS + (2 * chip_of[d] + parity) * RESP_ROWS
            at = pl.ds(pl.multiple_of(at, RESP_ROWS), RESP_ROWS)
            off = 2 * RESP_ROWS * d
            kk[at, 0:128] = resp_in[s][off : off + RESP_ROWS, :]
            vv[at, 0:128] = resp_in[s][off + RESP_ROWS : off + 2 * RESP_ROWS, :]
    kk[:, 128:256] = kk[:, 0:128]
    kT[...] = kk[:, 0:128].T
    vT[0:128, :] = vv[:, 0:128].T
    vT[128:144, :] = jnp.ones((16, KEYS), BF)
    lane = lax.broadcasted_iota(jnp.int32, (KEYS, 128), 1)
    vv[:, 128:256] = jnp.where(lane < 2, 1.0, 0.0).astype(BF)
    for j in range(4):
        for h in range(4):
            q = qs[j, :, h * 128 : (h + 1) * 128]
            r0 = j * 512 + h * 128
            qn[r0 : r0 + 128, :] = q
            qc = q.T.astype(F32) * SCALE_LOG2
            hi = qc.astype(BF)
            qT[0:128, r0 : r0 + 128] = hi
            qT[128:256, r0 : r0 + 128] = (qc - hi.astype(F32)).astype(BF)

    for j in range(4):
        w = 256 * (j + 1)
        n = PROMPT_KEYS + w
        cols = slice(j * 512, (j + 1) * 512)
        s = dot(kk[0 : n - 256, :], qT[:, cols])
        sp[0 : n - 256, :] = s
        top = jnp.max(s, axis=0, keepdims=True)
        s = dot(kk[n - 256 : n, :], qT[:, cols])
        row = c * 128 + lax.rem(lax.broadcasted_iota(jnp.int32, (256, 512), 1), 128)
        key = lax.broadcasted_iota(jnp.int32, (256, 512), 0)
        s = jnp.where(key <= row, s, -jnp.inf)
        sp[n - 256 : n, :] = s
        top = jnp.maximum(top, jnp.max(s, axis=0, keepdims=True))
        e = jnp.exp2(sp[0:n, :] - top).astype(BF)
        ee[0:n, cols] = e
        a = dot(vT[:, 0:n], e)
        inv = 1.0 / a[128:129, :]
        lane = lax.broadcasted_iota(jnp.int32, (1, 512), 1)
        live = (2 * j + c) * 128 + lax.rem(lane, 128) < length
        oT = jnp.where(live, a[0:128, :] * inv, 0.0).astype(BF)
        for h in range(4):
            hs = slice(h * 128, (h + 1) * 128)
            r0 = j * 512 + h * 128
            o = oT[:, hs]
            os_[j, :, hs] = o.T
            gt = jnp.where(live[:, hs], gs[j, :, hs].T.astype(F32) * inv[:, hs], 0.0).astype(BF)
            row_dot = jnp.sum(gt.astype(F32) * o.astype(F32), axis=0, keepdims=True)
            gT[0:128, r0 : r0 + 128] = gt
            gn[r0 : r0 + 128, :] = gt.T
            high = row_dot.astype(BF).astype(F32)
            sub = lax.broadcasted_iota(jnp.int32, (128, 128), 0)
            gT[128:256, r0 : r0 + 128] = jnp.where(
                sub == 0, -high, jnp.where(sub == 1, high - row_dot, 0.0)
            ).astype(BF)

    def prompt_block(t, _):
        keys = pl.ds(pl.multiple_of(t * KEY_BLOCK, KEY_BLOCK), KEY_BLOCK)
        dp = dot(vv[keys, :], gT[...])
        ds_s[...] = (dp * ee[keys, :].astype(F32)).astype(BF)
        dvp[keys, :] = dot(ee[keys, :], gn[...])
        dkp[keys, :] = dot(ds_s[...], qn[...]) * SCALE
        part = dot(kT[:, keys], ds_s[...])

        @pl.when(t == 0)
        def _():
            dq[...] = part

        @pl.when(t > 0)
        def _():
            dq[...] += part

        return 0

    lax.fori_loop(0, PROMPT_KEYS // KEY_BLOCK, prompt_block, 0)
    for t in range(4):
        keys = slice(PROMPT_KEYS + 256 * t, PROMPT_KEYS + 256 * (t + 1))
        at = slice(256 * t, 256 * (t + 1))
        cols = slice(512 * t, 2048)
        e = ee[keys, cols]
        ds = (dot(vv[keys, :], gT[:, cols]) * e.astype(F32)).astype(BF)
        dvr[at, :] = dot(e, gn[cols, :])
        dkr[at, :] = dot(ds, qn[cols, :]) * SCALE
        dq[:, cols] += dot(kT[:, keys], ds)

    for s in range(4):
        for d in range(CHIPS):
            at = slice(768 * s + PROMPT_ROWS * d, 768 * s + PROMPT_ROWS * (d + 1))
            off = 2 * PROMPT_ROWS * d
            out = dprompt_out[s]
            out[off : off + PROMPT_ROWS, :] = dkp[at, :].astype(out.dtype)
            out[off + PROMPT_ROWS : off + 2 * PROMPT_ROWS, :] = dvp[at, :].astype(out.dtype)
    for s in range(2):
        for d in range(CHIPS):
            parity = c if s == 0 else 1 - c
            at = (2 * chip_of[d] + parity) * RESP_ROWS
            at = pl.ds(pl.multiple_of(at, RESP_ROWS), RESP_ROWS)
            off = 2 * RESP_ROWS * d
            out = dresp_out[s]
            out[off : off + RESP_ROWS, :] = dkr[at, :].astype(out.dtype)
            out[off + RESP_ROWS : off + 2 * RESP_ROWS, :] = dvr[at, :].astype(out.dtype)
    for j in range(4):
        for h in range(4):
            r0 = j * 512 + h * 128
            qs[j, :, h * 128 : (h + 1) * 128] = (dq[:, r0 : r0 + 128] * SCALE).T.astype(BF)
    for d in range(CHIPS):
        o_out[d][...] = os_[pl.ds(chip_of[d], 1)][0]
        dq_out[d][...] = qs[pl.ds(chip_of[d], 1)][0]


def to_chip(a, d):
    return lax.ppermute(
        a, "ctx", [(2 * x + c, 2 * ((x + d) % CHIPS) + c) for x in range(CHIPS) for c in range(2)]
    )


def to_core(a):
    return lax.ppermute(a, "ctx", [(i, i ^ 1) for i in range(2 * CHIPS)])


def to_pair(a):
    return lax.ppermute(a, "pair", [(0, 1), (1, 0)])


def spread(parts, sign):
    return [parts[0]] + [to_chip(parts[d], sign * d) for d in range(1, CHIPS)]


def small(body, name, out_shape, n_in, scalars=True, limit=24):
    return pl.pallas_call(
        body,
        out_shape=out_shape,
        in_specs=([SMEM] if scalars else []) + [VMEM] * n_in,
        out_specs=[VMEM] * len(out_shape),
        compiler_params=pltpu.CompilerParams(vmem_limit_bytes=limit << 20),
        name=name,
    )


def per_device(prompt_keys, prompt_values, resp_queries, resp_keys, resp_values, out_grad, lengths):
    ctx = lax.axis_index("ctx")
    place = jnp.stack([ctx % 2, lengths[0], ctx // 2]).astype(jnp.int32)
    block = shape((2 * PROMPT_ROWS, 128))
    rblock = shape((2 * RESP_ROWS, 128))
    rows = shape((RESP_ROWS, 512))

    packed = small(pack_keys, "pack_keys", [block] * 4 + [rblock] * 4, 4)(
        place, prompt_keys, prompt_values, resp_keys[0], resp_values[0]
    )
    pkv = spread(packed[:4], 1)
    rkv = spread(packed[4:], 1)
    packed = small(pack_rows, "pack_rows", [rows] * 8, 2)(place, resp_queries[0], out_grad[0])
    qs = spread(packed[:4], 1)
    gs = spread(packed[4:], 1)

    here = jnp.concatenate(pkv, axis=0)
    there = to_pair(here)
    resp = jnp.concatenate(rkv, axis=0)
    prompt = [here, to_core(here), there, to_core(there)]
    resps = [resp, to_core(resp)]

    all_rows = 4 * 512
    outs = pl.pallas_call(
        attention,
        out_shape=[rows] * 8
        + [shape((1536, 128), F32), shape((1536, 128)), shape((1536, 128), F32), shape((1536, 128))]
        + [shape((1024, 128), F32), shape((1024, 128))],
        in_specs=[SMEM] + [VMEM] * 14,
        out_specs=[VMEM] * 14,
        scratch_shapes=[
            pltpu.VMEM((4, 128, 512), BF),
            pltpu.VMEM((4, 128, 512), BF),
            pltpu.VMEM((4, 128, 512), BF),
            pltpu.VMEM((all_rows, 128), BF),
            pltpu.VMEM((256, all_rows), BF),
            pltpu.VMEM((256, all_rows), BF),
            pltpu.VMEM((all_rows, 128), BF),
            pltpu.VMEM((KEYS, 256), BF),
            pltpu.VMEM((128, KEYS), BF),
            pltpu.VMEM((KEYS, 256), BF),
            pltpu.VMEM((144, KEYS), BF),
            pltpu.VMEM((KEYS, 512), F32),
            pltpu.VMEM((KEYS, all_rows), BF),
            pltpu.VMEM((KEY_BLOCK, all_rows), BF),
            pltpu.VMEM((128, all_rows), F32),
            pltpu.VMEM((PROMPT_KEYS, 128), F32),
            pltpu.VMEM((PROMPT_KEYS, 128), F32),
            pltpu.VMEM((1024, 128), F32),
            pltpu.VMEM((1024, 128), F32),
        ],
        compiler_params=pltpu.CompilerParams(vmem_limit_bytes=60 << 20),
        cost_estimate=pl.CostEstimate(
            flops=10 * 2048 * 3712 * 128, bytes_accessed=10 << 20, transcendentals=2048 * 3712
        ),
        name="attention",
    )(place, *qs, *gs, *prompt, *resps)
    o, dq = outs[0:4], outs[4:8]
    d_here, d_here_other, d_there, d_there_other, d_resp, d_resp_other = outs[8:14]

    got_there = to_core(d_there_other)
    far = (d_there + got_there.astype(F32)).astype(BF)
    got_far = to_pair(far)
    got_here = to_core(d_here_other)
    got_resp = to_core(d_resp_other)
    dr = small(sum_resp, "sum_resp", [rblock] * 4, 2, False)(d_resp, got_resp)
    dr = spread(dr, -1)
    o = spread(o, -1)
    dq = spread(dq, -1)
    dp = small(sum_prompt, "sum_prompt", [block] * 4, 3, False)(d_here, got_here, got_far)
    dp = spread(dp, -1)
    attn_out, query_grad = small(unpack_rows, "unpack_rows", [shape((128, 2048))] * 2, 8)(
        place, *o, *dq
    )
    pk, pv, rk, rv = small(
        unpack_keys, "unpack_keys", [shape((192, 512))] * 2 + [shape((128, 512))] * 2, 8
    )(place, *dp, *dr)
    return attn_out[None], query_grad[None], rk[None], rv[None], pk, pv


def solution(mesh):
    placed = (
        P(("batch", "pair", "ctx"), None),
        P(("batch", "pair", "ctx"), None),
        P("pair", ("batch", "ctx"), None),
        P("pair", ("batch", "ctx"), None),
        P("pair", ("batch", "ctx"), None),
        P("pair", ("batch", "ctx"), None),
        P(("batch", "pair")),
    )
    return jax.shard_map(
        per_device,
        mesh=mesh,
        in_specs=placed,
        out_specs=(
            P("pair", ("batch", "ctx"), None),
            P("pair", ("batch", "ctx"), None),
            P("pair", ("batch", "ctx"), None),
            P("pair", ("batch", "ctx"), None),
            P(("batch", "pair", "ctx"), None),
            P(("batch", "pair", "ctx"), None),
        ),
        check_vma=False,
    )
```

```python
import math

import jax
import jax.numpy as jnp
from jax import lax
from jax.experimental import pallas as pl
from jax.experimental.pallas import tpu as pltpu
from jax.sharding import PartitionSpec as P

F32 = jnp.float32
BF = jnp.bfloat16
SCALE = 1.0 / math.sqrt(128.0)
SCALE_LOG2 = math.log2(math.e) / math.sqrt(128.0)
CHIPS = 4
PROMPT_ROWS = 192
RESP_ROWS = 128
KEYS = 4096
PROMPT_KEYS = 3072
KEY_BLOCK = 1536
VMEM = pl.BlockSpec(memory_space=pltpu.VMEM)
SMEM = pl.BlockSpec(memory_space=pltpu.SMEM)


def dot(a, b):
    return jnp.dot(a, b, preferred_element_type=F32)


def shape(dims, dtype=BF):
    return jax.ShapeDtypeStruct(dims, dtype)


def lanes(index, width):
    return pl.ds(pl.multiple_of(index * width, width), width)


def pack_keys(place, pk, pv, rk, rv, *outs):
    x = place[2]
    for d in range(CHIPS):
        head = lanes(lax.rem(x + d, CHIPS), 128)
        outs[d][0:192, :] = pk[:, head]
        outs[d][192:384, :] = pv[:, head]
        outs[d][384:512, :] = rk[:, head]
        outs[d][512:640, :] = rv[:, head]


def pack_rows(place, q, g, *outs):
    x = place[2]
    for d in range(CHIPS):
        heads = lanes(lax.rem(x + d, CHIPS), 512)
        outs[d][0:128, :] = q[:, heads]
        outs[d][128:256, :] = g[:, heads]


def unpack_rows(place, *refs):
    x = place[2]
    oq, o, dq = refs[0:4], refs[4], refs[5]
    for d in range(CHIPS):
        heads = lanes(lax.rem(x + d, CHIPS), 512)
        o[:, heads] = oq[d][0:128, :]
        dq[:, heads] = oq[d][128:256, :]


def unpack_keys(place, *refs):
    x = place[2]
    pk, pv, rk, rv = refs[2 * CHIPS :]
    for d in range(CHIPS):
        head = lanes(lax.rem(x + d, CHIPS), 128)
        pk[:, head] = refs[d][0:PROMPT_ROWS, :]
        pv[:, head] = refs[d][PROMPT_ROWS:, :]
        rk[:, head] = refs[CHIPS + d][0:RESP_ROWS, :]
        rv[:, head] = refs[CHIPS + d][RESP_ROWS:, :]


def sum_prompt(own, other, far, *outs):
    for d in range(CHIPS):
        at = slice(384 * d, 384 * (d + 1))
        outs[d][...] = (own[at, :] + other[at, :].astype(F32) + far[at, :].astype(F32)).astype(BF)


def sum_resp(own, other, *outs):
    for d in range(CHIPS):
        at = slice(256 * d, 256 * (d + 1))
        far = slice(1536 + 256 * d, 1792 + 256 * d)
        outs[d][...] = (own[at, :] + other[far, :].astype(F32)).astype(BF)


def attention(place, *refs):
    qg_in = refs[0:4]
    own_in, other_in = refs[4:6]
    prompt_in = (own_in, other_in, refs[6], refs[7])
    oq_out = refs[8:12]
    own_out, resp_out, other_out = refs[12:15]
    dprompt_out = (own_out, other_out, refs[15], refs[16])
    (qs, gs, os_, qn, qT, gT, gn, kk, kT, vv, vT, sp, ee, ds_s, dq, dkp, dvp, dkr, dvr) = refs[17:]
    c, length, x = place[0], place[1], place[2]

    chip_of = [lax.rem(x + CHIPS - d, CHIPS) for d in range(CHIPS)]
    for d in range(CHIPS):
        qs[pl.ds(chip_of[d], 1)] = qg_in[d][0:128, :][None]
        gs[pl.ds(chip_of[d], 1)] = qg_in[d][128:256, :][None]
    for s in range(4):
        for d in range(CHIPS):
            at = slice(768 * s + PROMPT_ROWS * d, 768 * s + PROMPT_ROWS * (d + 1))
            off = 2 * PROMPT_ROWS * d
            kk[at, 0:128] = prompt_in[s][off : off + PROMPT_ROWS, :]
            vv[at, 0:128] = prompt_in[s][off + PROMPT_ROWS : off + 2 * PROMPT_ROWS, :]
    resp_at = []
    for s in range(2):
        for d in range(CHIPS):
            parity = c if s == 0 else 1 - c
            at = PROMPT_KEYS + (2 * chip_of[d] + parity) * RESP_ROWS
            at = pl.ds(pl.multiple_of(at, RESP_ROWS), RESP_ROWS)
            off = 1536 + 2 * RESP_ROWS * d
            kk[at, 0:128] = prompt_in[s][off : off + RESP_ROWS, :]
            vv[at, 0:128] = prompt_in[s][off + RESP_ROWS : off + 2 * RESP_ROWS, :]
    kk[:, 128:256] = kk[:, 0:128]
    kT[...] = kk[:, 0:128].T
    vT[0:128, :] = vv[:, 0:128].T
    vT[128:144, :] = jnp.ones((16, KEYS), BF)
    lane = lax.broadcasted_iota(jnp.int32, (KEYS, 128), 1)
    vv[:, 128:256] = jnp.where(lane < 2, 1.0, 0.0).astype(BF)
    for j in range(4):
        for h in range(4):
            q = qs[j, :, h * 128 : (h + 1) * 128]
            r0 = j * 512 + h * 128
            qn[r0 : r0 + 128, :] = q
            qc = q.T.astype(F32) * SCALE_LOG2
            hi = qc.astype(BF)
            qT[0:128, r0 : r0 + 128] = hi
            qT[128:256, r0 : r0 + 128] = (qc - hi.astype(F32)).astype(BF)

    def chunks(j):
        return [(512 * t, 512 * (t + 1)) for t in range(PROMPT_KEYS // 512)] + [
            (PROMPT_KEYS + 256 * t, PROMPT_KEYS + 256 * (t + 1)) for t in range(j + 1)
        ]

    tops, sums = [None] * 4, [None] * 4
    for j in range(5):
        now = chunks(j) if j < 4 else []
        before = chunks(j - 1) if j > 0 else []
        cols = slice(j * 512, (j + 1) * 512)
        cols_before = slice((j - 1) * 512, j * 512)
        for n in range(max(len(now), len(before))):
            if n < len(now):
                lo, hi = now[n]
                s = dot(kk[lo:hi, :], qT[:, cols])
                if n == len(now) - 1:
                    row = c * 128 + lax.rem(lax.broadcasted_iota(jnp.int32, (256, 512), 1), 128)
                    key = lax.broadcasted_iota(jnp.int32, (256, 512), 0)
                    s = jnp.where(key <= row, s, -jnp.inf)
                sp[j % 2, lo:hi, :] = s
                top = jnp.max(s, axis=0, keepdims=True)
                tops[j] = top if n == 0 else jnp.maximum(tops[j], top)
            if n < len(before):
                lo, hi = before[n]
                e = jnp.exp2(sp[(j - 1) % 2, lo:hi, :] - tops[j - 1]).astype(BF)
                ee[lo:hi, cols_before] = e
                part = dot(vT[:, lo:hi], e)
                sums[j - 1] = part if n == 0 else sums[j - 1] + part
    for j in range(4):
        a = sums[j]
        inv = 1.0 / a[128:129, :]
        lane = lax.broadcasted_iota(jnp.int32, (1, 512), 1)
        live = (2 * j + c) * 128 + lax.rem(lane, 128) < length
        oT = jnp.where(live, a[0:128, :] * inv, 0.0).astype(BF)
        for h in range(4):
            hs = slice(h * 128, (h + 1) * 128)
            r0 = j * 512 + h * 128
            o = oT[:, hs]
            os_[j, :, hs] = o.T
            gt = jnp.where(live[:, hs], gs[j, :, hs].T.astype(F32) * inv[:, hs], 0.0).astype(BF)
            row_dot = jnp.sum(gt.astype(F32) * o.astype(F32), axis=0, keepdims=True)
            gT[0:128, r0 : r0 + 128] = gt
            gn[r0 : r0 + 128, :] = gt.T
            high = row_dot.astype(BF).astype(F32)
            sub = lax.broadcasted_iota(jnp.int32, (128, 128), 0)
            gT[128:256, r0 : r0 + 128] = jnp.where(
                sub == 0, -high, jnp.where(sub == 1, high - row_dot, 0.0)
            ).astype(BF)

    def prompt_block(t, _):
        keys = pl.ds(pl.multiple_of(t * KEY_BLOCK, KEY_BLOCK), KEY_BLOCK)
        dp = dot(vv[keys, :], gT[...])
        ds_s[...] = (dp * ee[keys, :].astype(F32)).astype(BF)
        dvp[keys, :] = dot(ee[keys, :], gn[...])
        dkp[keys, :] = dot(ds_s[...], qn[...]) * SCALE
        part = dot(kT[:, keys], ds_s[...])

        @pl.when(t == 0)
        def _():
            dq[...] = part

        @pl.when(t > 0)
        def _():
            dq[...] += part

        return 0

    lax.fori_loop(0, PROMPT_KEYS // KEY_BLOCK, prompt_block, 0)
    for t in range(4):
        keys = slice(PROMPT_KEYS + 256 * t, PROMPT_KEYS + 256 * (t + 1))
        at = slice(256 * t, 256 * (t + 1))
        cols = slice(512 * t, 2048)
        e = ee[keys, cols]
        ds = (dot(vv[keys, :], gT[:, cols]) * e.astype(F32)).astype(BF)
        dvr[at, :] = dot(e, gn[cols, :])
        dkr[at, :] = dot(ds, qn[cols, :]) * SCALE
        dq[:, cols] += dot(kT[:, keys], ds)

    for s in range(4):
        for d in range(CHIPS):
            at = slice(768 * s + PROMPT_ROWS * d, 768 * s + PROMPT_ROWS * (d + 1))
            off = 2 * PROMPT_ROWS * d
            out = dprompt_out[s]
            out[off : off + PROMPT_ROWS, :] = dkp[at, :].astype(out.dtype)
            out[off + PROMPT_ROWS : off + 2 * PROMPT_ROWS, :] = dvp[at, :].astype(out.dtype)
    for s in range(2):
        for d in range(CHIPS):
            parity = c if s == 0 else 1 - c
            at = (2 * chip_of[d] + parity) * RESP_ROWS
            at = pl.ds(pl.multiple_of(at, RESP_ROWS), RESP_ROWS)
            off = 2 * RESP_ROWS * d + (1536 if s else 0)
            out = other_out if s else resp_out
            out[off : off + RESP_ROWS, :] = dkr[at, :].astype(out.dtype)
            out[off + RESP_ROWS : off + 2 * RESP_ROWS, :] = dvr[at, :].astype(out.dtype)
    for j in range(4):
        for h in range(4):
            r0 = j * 512 + h * 128
            qs[j, :, h * 128 : (h + 1) * 128] = (dq[:, r0 : r0 + 128] * SCALE).astype(BF).T
    for d in range(CHIPS):
        oq_out[d][0:128, :] = os_[pl.ds(chip_of[d], 1)][0]
        oq_out[d][128:256, :] = qs[pl.ds(chip_of[d], 1)][0]


def to_chip(a, d):
    return lax.ppermute(
        a, "ctx", [(2 * x + c, 2 * ((x + d) % CHIPS) + c) for x in range(CHIPS) for c in range(2)]
    )


def to_core(a):
    return lax.ppermute(a, "ctx", [(i, i ^ 1) for i in range(2 * CHIPS)])


def to_pair(a):
    return lax.ppermute(a, "pair", [(0, 1), (1, 0)])


def spread(parts, sign):
    return [parts[0]] + [to_chip(parts[d], sign * d) for d in range(1, CHIPS)]


def small(body, name, out_shape, n_in, scalars=True, limit=24):
    return pl.pallas_call(
        body,
        out_shape=out_shape,
        in_specs=([SMEM] if scalars else []) + [VMEM] * n_in,
        out_specs=[VMEM] * len(out_shape),
        compiler_params=pltpu.CompilerParams(vmem_limit_bytes=limit << 20),
        name=name,
    )


def per_device(prompt_keys, prompt_values, resp_queries, resp_keys, resp_values, out_grad, lengths):
    ctx = lax.axis_index("ctx")
    place = jnp.stack([ctx % 2, lengths[0], ctx // 2]).astype(jnp.int32)
    block = shape((640, 128))
    rows = shape((256, 512))
    far_block = (1536, 128)
    own_block = (2560, 128)

    packed = small(pack_keys, "pack_keys", [block] * 4, 4)(
        place, prompt_keys, prompt_values, resp_keys[0], resp_values[0]
    )
    kv = spread(packed, 1)
    packed = small(pack_rows, "pack_rows", [rows] * 4, 2)(place, resp_queries[0], out_grad[0])
    prompt = jnp.concatenate([k[:384] for k in kv], axis=0)
    own = jnp.concatenate([k[:384] for k in kv] + [k[384:] for k in kv], axis=0)
    far = to_pair(prompt)
    other = to_core(own)
    sent = lax.optimization_barrier(tuple(packed) + (prompt,))
    qg = spread(sent[:4], 1)
    held = lax.optimization_barrier((far, *qg))
    far, qg = held[0], held[1:]
    far_other = to_core(far)

    all_rows = 4 * 512
    outs = pl.pallas_call(
        attention,
        out_shape=[rows] * 4
        + [shape(far_block, F32), shape((1024, 128), F32), shape(own_block)]
        + [shape(far_block, F32), shape(far_block)],
        in_specs=[SMEM] + [VMEM] * 8,
        out_specs=[VMEM] * 9,
        scratch_shapes=[
            pltpu.VMEM((4, 128, 512), BF),
            pltpu.VMEM((4, 128, 512), BF),
            pltpu.VMEM((4, 128, 512), BF),
            pltpu.VMEM((all_rows, 128), BF),
            pltpu.VMEM((256, all_rows), BF),
            pltpu.VMEM((256, all_rows), BF),
            pltpu.VMEM((all_rows, 128), BF),
            pltpu.VMEM((KEYS, 256), BF),
            pltpu.VMEM((128, KEYS), BF),
            pltpu.VMEM((KEYS, 256), BF),
            pltpu.VMEM((144, KEYS), BF),
            pltpu.VMEM((2, KEYS, 512), F32),
            pltpu.VMEM((KEYS, all_rows), BF),
            pltpu.VMEM((KEY_BLOCK, all_rows), BF),
            pltpu.VMEM((128, all_rows), F32),
            pltpu.VMEM((PROMPT_KEYS, 128), F32),
            pltpu.VMEM((PROMPT_KEYS, 128), F32),
            pltpu.VMEM((1024, 128), F32),
            pltpu.VMEM((1024, 128), F32),
        ],
        compiler_params=pltpu.CompilerParams(vmem_limit_bytes=60 << 20),
        cost_estimate=pl.CostEstimate(
            flops=10 * 2048 * 3712 * 128, bytes_accessed=10 << 20, transcendentals=2048 * 3712
        ),
        name="attention",
    )(place, *qg, own, other, far, far_other)
    oq = outs[0:4]
    d_own, d_resp, d_other, d_far, d_far_other = outs[4:9]

    got_far = to_core(d_far_other)
    got_other = to_core(d_other)
    oq = spread(oq, -1)
    there = (d_far + got_far.astype(F32)).astype(BF)
    here = to_pair(there)
    dr = small(sum_resp, "sum_resp", [shape((256, 128))] * 4, 2, False)(d_resp, got_other)
    dr = spread(dr, -1)
    dp = small(sum_prompt, "sum_prompt", [shape((384, 128))] * 4, 3, False)(d_own, got_other, here)
    dp = spread(dp, -1)
    attn_out, query_grad = small(unpack_rows, "unpack_rows", [shape((128, 2048))] * 2, 4)(
        place, *oq
    )
    pk, pv, rk, rv = small(
        unpack_keys, "unpack_keys", [shape((192, 512))] * 2 + [shape((128, 512))] * 2, 8
    )(place, *dp, *dr)
    return attn_out[None], query_grad[None], rk[None], rv[None], pk, pv


def solution(mesh):
    placed = (
        P(("batch", "pair", "ctx"), None),
        P(("batch", "pair", "ctx"), None),
        P("pair", ("batch", "ctx"), None),
        P("pair", ("batch", "ctx"), None),
        P("pair", ("batch", "ctx"), None),
        P("pair", ("batch", "ctx"), None),
        P(("batch", "pair")),
    )
    return jax.shard_map(
        per_device,
        mesh=mesh,
        in_specs=placed,
        out_specs=(
            P("pair", ("batch", "ctx"), None),
            P("pair", ("batch", "ctx"), None),
            P("pair", ("batch", "ctx"), None),
            P("pair", ("batch", "ctx"), None),
            P(("batch", "pair", "ctx"), None),
            P(("batch", "pair", "ctx"), None),
        ),
        check_vma=False,
    )
```

```python
import math

import jax
import jax.numpy as jnp
from jax import lax
from jax.experimental import pallas as pl
from jax.experimental.pallas import tpu as pltpu
from jax.sharding import PartitionSpec as P

F32 = jnp.float32
BF = jnp.bfloat16
SCALE = 1.0 / math.sqrt(128.0)
SCALE_LOG2 = math.log2(math.e) / math.sqrt(128.0)
CHIPS = 4
PROMPT_ROWS = 192
RESP_ROWS = 128
KEYS = 4096
PROMPT_KEYS = 3072
KEY_BLOCK = 1536
VMEM = pl.BlockSpec(memory_space=pltpu.VMEM)
SMEM = pl.BlockSpec(memory_space=pltpu.SMEM)


def dot(a, b):
    return jnp.dot(a, b, preferred_element_type=F32)


def shape(dims, dtype=BF):
    return jax.ShapeDtypeStruct(dims, dtype)


def lanes(index, width):
    return pl.ds(pl.multiple_of(index * width, width), width)


def pack_keys(place, pk, pv, rk, rv, *refs):
    x = place[2]
    sems = refs[4]
    copies = []
    for d in range(CHIPS):
        head = lanes(lax.rem(x + d, CHIPS), 128)
        for src, lo, hi in ((pk, 0, 192), (pv, 192, 384), (rk, 384, 512), (rv, 512, 640)):
            copies.append(
                pltpu.make_async_copy(
                    src.at[:, head], refs[d].at[lo:hi, :], sems.at[len(copies)]
                )
            )
    for copy in copies:
        copy.start()
    for copy in copies:
        copy.wait()


def pack_rows(place, q, g, *outs):
    x = place[2]
    for d in range(CHIPS):
        heads = lanes(lax.rem(x + d, CHIPS), 512)
        outs[d][0:128, :] = q[:, heads]
        outs[d][128:256, :] = g[:, heads]


def unpack_rows(place, *refs):
    x = place[2]
    oq, o, dq = refs[0:4], refs[4], refs[5]
    for d in range(CHIPS):
        heads = lanes(lax.rem(x + d, CHIPS), 512)
        o[:, heads] = oq[d][0:128, :]
        dq[:, heads] = oq[d][128:256, :]


def unpack_keys(place, *refs):
    x = place[2]
    pk, pv, rk, rv = refs[2 * CHIPS :]
    for d in range(CHIPS):
        head = lanes(lax.rem(x + d, CHIPS), 128)
        pk[:, head] = refs[d][0:PROMPT_ROWS, :]
        pv[:, head] = refs[d][PROMPT_ROWS:, :]
        rk[:, head] = refs[CHIPS + d][0:RESP_ROWS, :]
        rv[:, head] = refs[CHIPS + d][RESP_ROWS:, :]


def sum_prompt(own, other, far, *outs):
    for d in range(CHIPS):
        at = slice(384 * d, 384 * (d + 1))
        outs[d][...] = (own[at, :] + other[at, :].astype(F32) + far[at, :].astype(F32)).astype(BF)


def sum_resp(own, other, *outs):
    for d in range(CHIPS):
        at = slice(256 * d, 256 * (d + 1))
        far = slice(1536 + 256 * d, 1792 + 256 * d)
        outs[d][...] = (own[at, :] + other[far, :].astype(F32)).astype(BF)


def attention(place, *refs):
    qg_in = refs[0:4]
    own_in, other_in = refs[4:6]
    prompt_in = (own_in, other_in, refs[6], refs[7])
    oq_out = refs[8:12]
    own_out, resp_out, other_out = refs[12:15]
    dprompt_out = (own_out, other_out, refs[15], refs[16])
    (qs, gs, os_, qn, qT, gT, gn, kk, kT, vv, vT, sp, ee, dq, dkp, dvp, dkr, dvr) = refs[17:]
    c, length, x = place[0], place[1], place[2]

    chip_of = [lax.rem(x + CHIPS - d, CHIPS) for d in range(CHIPS)]
    for d in range(CHIPS):
        qs[pl.ds(chip_of[d], 1)] = qg_in[d][0:128, :][None]
        gs[pl.ds(chip_of[d], 1)] = qg_in[d][128:256, :][None]
    for s in range(4):
        for d in range(CHIPS):
            at = slice(768 * s + PROMPT_ROWS * d, 768 * s + PROMPT_ROWS * (d + 1))
            off = 2 * PROMPT_ROWS * d
            kk[at, 0:128] = prompt_in[s][off : off + PROMPT_ROWS, :]
            vv[at, 0:128] = prompt_in[s][off + PROMPT_ROWS : off + 2 * PROMPT_ROWS, :]
    resp_at = []
    for s in range(2):
        for d in range(CHIPS):
            parity = c if s == 0 else 1 - c
            at = PROMPT_KEYS + (2 * chip_of[d] + parity) * RESP_ROWS
            at = pl.ds(pl.multiple_of(at, RESP_ROWS), RESP_ROWS)
            off = 1536 + 2 * RESP_ROWS * d
            kk[at, 0:128] = prompt_in[s][off : off + RESP_ROWS, :]
            vv[at, 0:128] = prompt_in[s][off + RESP_ROWS : off + 2 * RESP_ROWS, :]
    kk[:, 128:256] = kk[:, 0:128]
    kT[...] = kk[:, 0:128].T
    vT[0:128, :] = vv[:, 0:128].T
    vT[128:144, :] = jnp.ones((16, KEYS), BF)
    lane = lax.broadcasted_iota(jnp.int32, (KEYS, 128), 1)
    vv[:, 128:256] = jnp.where(lane < 2, 1.0, 0.0).astype(BF)
    for j in range(4):
        for h in range(4):
            q = qs[j, :, h * 128 : (h + 1) * 128]
            r0 = j * 512 + h * 128
            qn[r0 : r0 + 128, :] = q
            qc = q.T.astype(F32) * SCALE_LOG2
            hi = qc.astype(BF)
            qT[0:128, r0 : r0 + 128] = hi
            qT[128:256, r0 : r0 + 128] = (qc - hi.astype(F32)).astype(BF)

    def chunks(j):
        return [(512 * t, 512 * (t + 1)) for t in range(PROMPT_KEYS // 512)] + [
            (PROMPT_KEYS + 256 * t, PROMPT_KEYS + 256 * (t + 1)) for t in range(j + 1)
        ]

    tops, sums = [None] * 4, [None] * 4
    for j in range(5):
        now = chunks(j) if j < 4 else []
        before = chunks(j - 1) if j > 0 else []
        cols = slice(j * 512, (j + 1) * 512)
        cols_before = slice((j - 1) * 512, j * 512)
        for n in range(max(len(now), len(before))):
            if n < len(now):
                lo, hi = now[n]
                s = dot(kk[lo:hi, :], qT[:, cols])
                if n == len(now) - 1:
                    row = c * 128 + lax.rem(lax.broadcasted_iota(jnp.int32, (256, 512), 1), 128)
                    key = lax.broadcasted_iota(jnp.int32, (256, 512), 0)
                    s = jnp.where(key <= row, s, -jnp.inf)
                sp[j % 2, lo:hi, :] = s
                top = jnp.max(s, axis=0, keepdims=True)
                tops[j] = top if n == 0 else jnp.maximum(tops[j], top)
            if n < len(before):
                lo, hi = before[n]
                e = jnp.exp2(sp[(j - 1) % 2, lo:hi, :] - tops[j - 1]).astype(BF)
                ee[lo:hi, cols_before] = e
                part = dot(vT[:, lo:hi], e)
                sums[j - 1] = part if n == 0 else sums[j - 1] + part
    for j in range(4):
        a = sums[j]
        inv = 1.0 / a[128:129, :]
        lane = lax.broadcasted_iota(jnp.int32, (1, 512), 1)
        live = (2 * j + c) * 128 + lax.rem(lane, 128) < length
        oT = jnp.where(live, a[0:128, :] * inv, 0.0).astype(BF)
        for h in range(4):
            hs = slice(h * 128, (h + 1) * 128)
            r0 = j * 512 + h * 128
            o = oT[:, hs]
            os_[j, :, hs] = o.T
            gt = jnp.where(live[:, hs], gs[j, :, hs].T.astype(F32) * inv[:, hs], 0.0).astype(BF)
            row_dot = jnp.sum(gt.astype(F32) * o.astype(F32), axis=0, keepdims=True)
            gT[0:128, r0 : r0 + 128] = gt
            gn[r0 : r0 + 128, :] = gt.T
            high = row_dot.astype(BF).astype(F32)
            sub = lax.broadcasted_iota(jnp.int32, (128, 128), 0)
            gT[128:256, r0 : r0 + 128] = jnp.where(
                sub == 0, -high, jnp.where(sub == 1, high - row_dot, 0.0)
            ).astype(BF)

    def prompt_block(t, _):
        keys = pl.ds(pl.multiple_of(t * KEY_BLOCK, KEY_BLOCK), KEY_BLOCK)
        dp = dot(vv[keys, :], gT[...])
        dvp[keys, :] = dot(ee[keys, :], gn[...])
        ee[keys, :] = (dp * ee[keys, :].astype(F32)).astype(BF)
        dkp[keys, :] = dot(ee[keys, :], qn[...]) * SCALE
        part = dot(kT[:, keys], ee[keys, :])

        @pl.when(t == 0)
        def _():
            dq[...] = part

        @pl.when(t > 0)
        def _():
            dq[...] += part

        return 0

    lax.fori_loop(0, PROMPT_KEYS // KEY_BLOCK, prompt_block, 0)
    for t in range(4):
        keys = slice(PROMPT_KEYS + 256 * t, PROMPT_KEYS + 256 * (t + 1))
        at = slice(256 * t, 256 * (t + 1))
        cols = slice(512 * t, 2048)
        e = ee[keys, cols]
        ds = (dot(vv[keys, :], gT[:, cols]) * e.astype(F32)).astype(BF)
        dvr[at, :] = dot(e, gn[cols, :])
        dkr[at, :] = dot(ds, qn[cols, :]) * SCALE
        dq[:, cols] += dot(kT[:, keys], ds)

    for s in range(4):
        for d in range(CHIPS):
            at = slice(768 * s + PROMPT_ROWS * d, 768 * s + PROMPT_ROWS * (d + 1))
            off = 2 * PROMPT_ROWS * d
            out = dprompt_out[s]
            out[off : off + PROMPT_ROWS, :] = dkp[at, :].astype(out.dtype)
            out[off + PROMPT_ROWS : off + 2 * PROMPT_ROWS, :] = dvp[at, :].astype(out.dtype)
    for s in range(2):
        for d in range(CHIPS):
            parity = c if s == 0 else 1 - c
            at = (2 * chip_of[d] + parity) * RESP_ROWS
            at = pl.ds(pl.multiple_of(at, RESP_ROWS), RESP_ROWS)
            off = 2 * RESP_ROWS * d + (1536 if s else 0)
            out = other_out if s else resp_out
            out[off : off + RESP_ROWS, :] = dkr[at, :].astype(out.dtype)
            out[off + RESP_ROWS : off + 2 * RESP_ROWS, :] = dvr[at, :].astype(out.dtype)
    for j in range(4):
        for h in range(4):
            r0 = j * 512 + h * 128
            qs[j, :, h * 128 : (h + 1) * 128] = (dq[:, r0 : r0 + 128] * SCALE).astype(BF).T
    for d in range(CHIPS):
        oq_out[d][0:128, :] = os_[pl.ds(chip_of[d], 1)][0]
        oq_out[d][128:256, :] = qs[pl.ds(chip_of[d], 1)][0]


def to_chip(a, d):
    return lax.ppermute(
        a, "ctx", [(2 * x + c, 2 * ((x + d) % CHIPS) + c) for x in range(CHIPS) for c in range(2)]
    )


def to_core(a):
    return lax.ppermute(a, "ctx", [(i, i ^ 1) for i in range(2 * CHIPS)])


def to_pair(a):
    return lax.ppermute(a, "pair", [(0, 1), (1, 0)])


def spread(parts, sign):
    return [parts[0]] + [to_chip(parts[d], sign * d) for d in range(1, CHIPS)]


def small(body, name, out_shape, n_in, scalars=True, limit=24):
    return pl.pallas_call(
        body,
        out_shape=out_shape,
        in_specs=([SMEM] if scalars else []) + [VMEM] * n_in,
        out_specs=[VMEM] * len(out_shape),
        compiler_params=pltpu.CompilerParams(vmem_limit_bytes=limit << 20),
        name=name,
    )


def per_device(prompt_keys, prompt_values, resp_queries, resp_keys, resp_values, out_grad, lengths):
    ctx = lax.axis_index("ctx")
    place = jnp.stack([ctx % 2, lengths[0], ctx // 2]).astype(jnp.int32)
    block = shape((640, 128))
    rows = shape((256, 512))
    far_block = (1536, 128)
    own_block = (2560, 128)

    kv = pl.pallas_call(
        pack_keys,
        out_shape=[block] * 4,
        in_specs=[SMEM] + [pl.BlockSpec(memory_space=pltpu.HBM)] * 4,
        out_specs=[VMEM] * 4,
        scratch_shapes=[pltpu.SemaphoreType.DMA((16,))],
        name="pack_keys",
    )(place, prompt_keys, prompt_values, resp_keys[0], resp_values[0])
    kv = spread(kv, 1)
    packed = small(pack_rows, "pack_rows", [rows] * 4, 2)(place, resp_queries[0], out_grad[0])
    held = lax.optimization_barrier(tuple(packed) + tuple(kv))
    packed, kv = held[:4], held[4:]
    prompt = jnp.concatenate([k[:384] for k in kv], axis=0)
    own = jnp.concatenate([k[:384] for k in kv] + [k[384:] for k in kv], axis=0)
    far = to_pair(prompt)
    other = to_core(own)
    sent = lax.optimization_barrier(tuple(packed) + (prompt,))
    qg = spread(sent[:4], 1)
    held = lax.optimization_barrier((far, *qg))
    far, qg = held[0], held[1:]
    far_other = to_core(far)

    all_rows = 4 * 512
    outs = pl.pallas_call(
        attention,
        out_shape=[rows] * 4
        + [shape(far_block, F32), shape((1024, 128), F32), shape(own_block)]
        + [shape(far_block, F32), shape(far_block)],
        in_specs=[SMEM] + [VMEM] * 8,
        out_specs=[VMEM] * 9,
        scratch_shapes=[
            pltpu.VMEM((4, 128, 512), BF),
            pltpu.VMEM((4, 128, 512), BF),
            pltpu.VMEM((4, 128, 512), BF),
            pltpu.VMEM((all_rows, 128), BF),
            pltpu.VMEM((256, all_rows), BF),
            pltpu.VMEM((256, all_rows), BF),
            pltpu.VMEM((all_rows, 128), BF),
            pltpu.VMEM((KEYS, 256), BF),
            pltpu.VMEM((128, KEYS), BF),
            pltpu.VMEM((KEYS, 256), BF),
            pltpu.VMEM((144, KEYS), BF),
            pltpu.VMEM((2, KEYS, 512), F32),
            pltpu.VMEM((KEYS, all_rows), BF),
            pltpu.VMEM((128, all_rows), F32),
            pltpu.VMEM((PROMPT_KEYS, 128), F32),
            pltpu.VMEM((PROMPT_KEYS, 128), F32),
            pltpu.VMEM((1024, 128), F32),
            pltpu.VMEM((1024, 128), F32),
        ],
        compiler_params=pltpu.CompilerParams(vmem_limit_bytes=50 << 20),
        cost_estimate=pl.CostEstimate(
            flops=10 * 2048 * 3712 * 128, bytes_accessed=10 << 20, transcendentals=2048 * 3712
        ),
        name="attention",
    )(place, *qg, own, other, far, far_other)
    oq = outs[0:4]
    d_own, d_resp, d_other, d_far, d_far_other = outs[4:9]

    got_far = to_core(d_far_other)
    got_other = to_core(d_other)
    oq = spread(oq, -1)
    there = (d_far + got_far.astype(F32)).astype(BF)
    here = to_pair(there)
    dr = small(sum_resp, "sum_resp", [shape((256, 128))] * 4, 2, False)(d_resp, got_other)
    dr = spread(dr, -1)
    dp = small(sum_prompt, "sum_prompt", [shape((384, 128))] * 4, 3, False)(d_own, got_other, here)
    dp = spread(dp, -1)
    attn_out, query_grad = small(unpack_rows, "unpack_rows", [shape((128, 2048))] * 2, 4)(
        place, *oq
    )
    pk, pv, rk, rv = small(
        unpack_keys, "unpack_keys", [shape((192, 512))] * 2 + [shape((128, 512))] * 2, 8
    )(place, *dp, *dr)
    return attn_out[None], query_grad[None], rk[None], rv[None], pk, pv


def solution(mesh):
    placed = (
        P(("batch", "pair", "ctx"), None),
        P(("batch", "pair", "ctx"), None),
        P("pair", ("batch", "ctx"), None),
        P("pair", ("batch", "ctx"), None),
        P("pair", ("batch", "ctx"), None),
        P("pair", ("batch", "ctx"), None),
        P(("batch", "pair")),
    )
    return jax.shard_map(
        per_device,
        mesh=mesh,
        in_specs=placed,
        out_specs=(
            P("pair", ("batch", "ctx"), None),
            P("pair", ("batch", "ctx"), None),
            P("pair", ("batch", "ctx"), None),
            P("pair", ("batch", "ctx"), None),
            P(("batch", "pair", "ctx"), None),
            P(("batch", "pair", "ctx"), None),
        ),
        check_vma=False,
    )
```

```python
import math

import jax
import jax.numpy as jnp
from jax import lax
from jax.experimental import pallas as pl
from jax.experimental.pallas import tpu as pltpu
from jax.sharding import PartitionSpec as P

F32 = jnp.float32
BF = jnp.bfloat16
SCALE = 1.0 / math.sqrt(128.0)
SCALE_LOG2 = math.log2(math.e) / math.sqrt(128.0)
CHIPS = 4
PROMPT_ROWS = 192
RESP_ROWS = 128
KEYS = 4096
PROMPT_KEYS = 3072
KEY_BLOCK = 768
VMEM = pl.BlockSpec(memory_space=pltpu.VMEM)
SMEM = pl.BlockSpec(memory_space=pltpu.SMEM)


def dot(a, b):
    return jnp.dot(a, b, preferred_element_type=F32)


def shape(dims, dtype=BF):
    return jax.ShapeDtypeStruct(dims, dtype)


def lanes(index, width):
    return pl.ds(pl.multiple_of(index * width, width), width)


def pack_keys(place, pk, pv, rk, rv, *refs):
    x = place[2]
    sems = refs[4]
    copies = []
    for d in range(CHIPS):
        head = lanes(lax.rem(x + d, CHIPS), 128)
        for src, lo, hi in ((pk, 0, 192), (pv, 192, 384), (rk, 384, 512), (rv, 512, 640)):
            copies.append(
                pltpu.make_async_copy(
                    src.at[:, head], refs[d].at[lo:hi, :], sems.at[len(copies)]
                )
            )
    for copy in copies:
        copy.start()
    for copy in copies:
        copy.wait()


def pack_rows(place, q, g, *outs):
    x = place[2]
    for d in range(CHIPS):
        heads = lanes(lax.rem(x + d, CHIPS), 512)
        outs[d][0:128, :] = q[:, heads]
        outs[d][128:256, :] = g[:, heads]


def unpack_rows(place, *refs):
    x = place[2]
    oq, o, dq = refs[0:4], refs[4], refs[5]
    for d in range(CHIPS):
        heads = lanes(lax.rem(x + d, CHIPS), 512)
        o[:, heads] = oq[d][0:128, :]
        dq[:, heads] = oq[d][128:256, :]


def unpack_keys(place, *refs):
    x = place[2]
    pk, pv, rk, rv = refs[2 * CHIPS :]
    for d in range(CHIPS):
        head = lanes(lax.rem(x + d, CHIPS), 128)
        pk[:, head] = refs[d][0:PROMPT_ROWS, :]
        pv[:, head] = refs[d][PROMPT_ROWS:, :]
        rk[:, head] = refs[CHIPS + d][0:RESP_ROWS, :]
        rv[:, head] = refs[CHIPS + d][RESP_ROWS:, :]


def sum_prompt(own, other, far, *outs):
    for d in range(CHIPS):
        at = slice(384 * d, 384 * (d + 1))
        outs[d][...] = (own[at, :] + other[at, :].astype(F32) + far[at, :].astype(F32)).astype(BF)


def sum_resp(own, other, *outs):
    for d in range(CHIPS):
        at = slice(256 * d, 256 * (d + 1))
        far = slice(1536 + 256 * d, 1792 + 256 * d)
        outs[d][...] = (own[at, :] + other[far, :].astype(F32)).astype(BF)


def attention(place, *refs):
    qg_in = refs[0:4]
    own_in, other_in = refs[4:6]
    prompt_in = (own_in, other_in, refs[6], refs[7])
    oq_out = refs[8:12]
    own_out, resp_out, other_out = refs[12:15]
    dprompt_out = (own_out, other_out, refs[15], refs[16])
    (qs, gs, os_, qn, qT, gT, gn, kk, kT, vv, vT, sp, ee, dq, dkr, dvr) = refs[17:]
    c, length, x = place[0], place[1], place[2]

    chip_of = [lax.rem(x + CHIPS - d, CHIPS) for d in range(CHIPS)]
    for d in range(CHIPS):
        qs[pl.ds(chip_of[d], 1)] = qg_in[d][0:128, :][None]
        gs[pl.ds(chip_of[d], 1)] = qg_in[d][128:256, :][None]
    for s in range(4):
        for d in range(CHIPS):
            at = slice(768 * s + PROMPT_ROWS * d, 768 * s + PROMPT_ROWS * (d + 1))
            off = 2 * PROMPT_ROWS * d
            kk[at, 0:128] = prompt_in[s][off : off + PROMPT_ROWS, :]
            vv[at, 0:128] = prompt_in[s][off + PROMPT_ROWS : off + 2 * PROMPT_ROWS, :]
    resp_at = []
    for s in range(2):
        for d in range(CHIPS):
            parity = c if s == 0 else 1 - c
            at = PROMPT_KEYS + (2 * chip_of[d] + parity) * RESP_ROWS
            at = pl.ds(pl.multiple_of(at, RESP_ROWS), RESP_ROWS)
            off = 1536 + 2 * RESP_ROWS * d
            kk[at, 0:128] = prompt_in[s][off : off + RESP_ROWS, :]
            vv[at, 0:128] = prompt_in[s][off + RESP_ROWS : off + 2 * RESP_ROWS, :]
    kk[:, 128:256] = kk[:, 0:128]
    kT[...] = kk[:, 0:128].T
    vT[0:128, :] = vv[:, 0:128].T
    vT[128:144, :] = jnp.ones((16, KEYS), BF)
    lane = lax.broadcasted_iota(jnp.int32, (KEYS, 128), 1)
    vv[:, 128:256] = jnp.where(lane < 2, 1.0, 0.0).astype(BF)
    for j in range(4):
        for h in range(4):
            q = qs[j, :, h * 128 : (h + 1) * 128]
            r0 = j * 512 + h * 128
            qn[r0 : r0 + 128, :] = q
            qc = q.T.astype(F32) * SCALE_LOG2
            hi = qc.astype(BF)
            qT[0:128, r0 : r0 + 128] = hi
            qT[128:256, r0 : r0 + 128] = (qc - hi.astype(F32)).astype(BF)

    def chunks(j):
        return [(512 * t, 512 * (t + 1)) for t in range(PROMPT_KEYS // 512)] + [
            (PROMPT_KEYS + 256 * t, PROMPT_KEYS + 256 * (t + 1)) for t in range(j + 1)
        ]

    tops, sums = [None] * 8, [None] * 8
    for j in range(9):
        now = chunks(j // 2) if j < 8 else []
        before = chunks((j - 1) // 2) if j > 0 else []
        cols = slice(j * 256, (j + 1) * 256)
        cols_before = slice((j - 1) * 256, j * 256)
        for n in range(max(len(now), len(before))):
            if n < len(now):
                lo, hi = now[n]
                s = dot(kk[lo:hi, :], qT[:, cols])
                if n == len(now) - 1:
                    row = c * 128 + lax.rem(lax.broadcasted_iota(jnp.int32, (256, 256), 1), 128)
                    key = lax.broadcasted_iota(jnp.int32, (256, 256), 0)
                    s = jnp.where(key <= row, s, -jnp.inf)
                sp[j % 2, lo:hi, :] = s
                top = jnp.max(s, axis=0, keepdims=True)
                tops[j] = top if n == 0 else jnp.maximum(tops[j], top)
            if n < len(before):
                lo, hi = before[n]
                e = jnp.exp2(sp[(j - 1) % 2, lo:hi, :] - tops[j - 1]).astype(BF)
                ee[lo:hi, cols_before] = e
                part = dot(vT[:, lo:hi], e)
                sums[j - 1] = part if n == 0 else sums[j - 1] + part
    for j in range(4):
        a = jnp.concatenate([sums[2 * j], sums[2 * j + 1]], axis=1)
        inv = 1.0 / a[128:129, :]
        lane = lax.broadcasted_iota(jnp.int32, (1, 512), 1)
        live = (2 * j + c) * 128 + lax.rem(lane, 128) < length
        oT = jnp.where(live, a[0:128, :] * inv, 0.0).astype(BF)
        for h in range(4):
            hs = slice(h * 128, (h + 1) * 128)
            r0 = j * 512 + h * 128
            o = oT[:, hs]
            os_[j, :, hs] = o.T
            gt = jnp.where(live[:, hs], gs[j, :, hs].T.astype(F32) * inv[:, hs], 0.0).astype(BF)
            row_dot = jnp.sum(gt.astype(F32) * o.astype(F32), axis=0, keepdims=True)
            gT[0:128, r0 : r0 + 128] = gt
            gn[r0 : r0 + 128, :] = gt.T
            high = row_dot.astype(BF).astype(F32)
            sub = lax.broadcasted_iota(jnp.int32, (128, 128), 0)
            gT[128:256, r0 : r0 + 128] = jnp.where(
                sub == 0, -high, jnp.where(sub == 1, high - row_dot, 0.0)
            ).astype(BF)

    for t in range(PROMPT_KEYS // KEY_BLOCK):
        keys = slice(t * KEY_BLOCK, (t + 1) * KEY_BLOCK)
        dv = dot(ee[keys, :], gn[...])
        for j in range(4):
            cols = slice(j * 512, (j + 1) * 512)
            dp = dot(vv[keys, :], gT[:, cols])
            ee[keys, cols] = (dp * ee[keys, cols].astype(F32)).astype(BF)
        dk = dot(ee[keys, :], qn[...]) * SCALE
        out = dprompt_out[t]
        for d in range(CHIPS):
            at = slice(PROMPT_ROWS * d, PROMPT_ROWS * (d + 1))
            off = 2 * PROMPT_ROWS * d
            out[off : off + PROMPT_ROWS, :] = dk[at, :].astype(out.dtype)
            out[off + PROMPT_ROWS : off + 2 * PROMPT_ROWS, :] = dv[at, :].astype(out.dtype)
        part = dot(kT[:, keys], ee[keys, :])
        if t == 0:
            dq[...] = part
        else:
            dq[...] += part
    for t in range(4):
        keys = slice(PROMPT_KEYS + 256 * t, PROMPT_KEYS + 256 * (t + 1))
        at = slice(256 * t, 256 * (t + 1))
        cols = slice(512 * t, 2048)
        e = ee[keys, cols]
        ds = (dot(vv[keys, :], gT[:, cols]) * e.astype(F32)).astype(BF)
        dvr[at, :] = dot(e, gn[cols, :])
        dkr[at, :] = dot(ds, qn[cols, :]) * SCALE
        dq[:, cols] += dot(kT[:, keys], ds)

    for s in range(2):
        for d in range(CHIPS):
            parity = c if s == 0 else 1 - c
            at = (2 * chip_of[d] + parity) * RESP_ROWS
            at = pl.ds(pl.multiple_of(at, RESP_ROWS), RESP_ROWS)
            off = 2 * RESP_ROWS * d + (1536 if s else 0)
            out = other_out if s else resp_out
            out[off : off + RESP_ROWS, :] = dkr[at, :].astype(out.dtype)
            out[off + RESP_ROWS : off + 2 * RESP_ROWS, :] = dvr[at, :].astype(out.dtype)
    for j in range(4):
        for h in range(4):
            r0 = j * 512 + h * 128
            qs[j, :, h * 128 : (h + 1) * 128] = (dq[:, r0 : r0 + 128] * SCALE).astype(BF).T
    for d in range(CHIPS):
        oq_out[d][0:128, :] = os_[pl.ds(chip_of[d], 1)][0]
        oq_out[d][128:256, :] = qs[pl.ds(chip_of[d], 1)][0]


def to_chip(a, d):
    return lax.ppermute(
        a, "ctx", [(2 * x + c, 2 * ((x + d) % CHIPS) + c) for x in range(CHIPS) for c in range(2)]
    )


def to_core(a):
    return lax.ppermute(a, "ctx", [(i, i ^ 1) for i in range(2 * CHIPS)])


def to_pair(a):
    return lax.ppermute(a, "pair", [(0, 1), (1, 0)])


def spread(parts, sign):
    return [parts[0]] + [to_chip(parts[d], sign * d) for d in range(1, CHIPS)]


def small(body, name, out_shape, n_in, scalars=True, limit=24):
    return pl.pallas_call(
        body,
        out_shape=out_shape,
        in_specs=([SMEM] if scalars else []) + [VMEM] * n_in,
        out_specs=[VMEM] * len(out_shape),
        compiler_params=pltpu.CompilerParams(vmem_limit_bytes=limit << 20),
        name=name,
    )


def per_device(prompt_keys, prompt_values, resp_queries, resp_keys, resp_values, out_grad, lengths):
    ctx = lax.axis_index("ctx")
    place = jnp.stack([ctx % 2, lengths[0], ctx // 2]).astype(jnp.int32)
    block = shape((640, 128))
    rows = shape((256, 512))
    far_block = (1536, 128)
    own_block = (2560, 128)

    kv = pl.pallas_call(
        pack_keys,
        out_shape=[block] * 4,
        in_specs=[SMEM] + [pl.BlockSpec(memory_space=pltpu.HBM)] * 4,
        out_specs=[VMEM] * 4,
        scratch_shapes=[pltpu.SemaphoreType.DMA((16,))],
        name="pack_keys",
    )(place, prompt_keys, prompt_values, resp_keys[0], resp_values[0])
    kv = spread(kv, 1)
    packed = small(pack_rows, "pack_rows", [rows] * 4, 2)(place, resp_queries[0], out_grad[0])
    held = lax.optimization_barrier(tuple(packed) + tuple(kv))
    packed, kv = held[:4], held[4:]
    prompt = jnp.concatenate([k[:384] for k in kv], axis=0)
    own = jnp.concatenate([k[:384] for k in kv] + [k[384:] for k in kv], axis=0)
    far = to_pair(prompt)
    other = to_core(own)
    sent = lax.optimization_barrier(tuple(packed) + (prompt,))
    qg = spread(sent[:4], 1)
    held = lax.optimization_barrier((far, *qg))
    far, qg = held[0], held[1:]
    far_other = to_core(far)

    all_rows = 4 * 512
    outs = pl.pallas_call(
        attention,
        out_shape=[rows] * 4
        + [shape(far_block, F32), shape((1024, 128), F32), shape(own_block)]
        + [shape(far_block, F32), shape(far_block)],
        in_specs=[SMEM] + [VMEM] * 8,
        out_specs=[VMEM] * 9,
        scratch_shapes=[
            pltpu.VMEM((4, 128, 512), BF),
            pltpu.VMEM((4, 128, 512), BF),
            pltpu.VMEM((4, 128, 512), BF),
            pltpu.VMEM((all_rows, 128), BF),
            pltpu.VMEM((256, all_rows), BF),
            pltpu.VMEM((256, all_rows), BF),
            pltpu.VMEM((all_rows, 128), BF),
            pltpu.VMEM((KEYS, 256), BF),
            pltpu.VMEM((128, KEYS), BF),
            pltpu.VMEM((KEYS, 256), BF),
            pltpu.VMEM((144, KEYS), BF),
            pltpu.VMEM((2, KEYS, 256), F32),
            pltpu.VMEM((KEYS, all_rows), BF),
            pltpu.VMEM((128, all_rows), F32),
            pltpu.VMEM((1024, 128), F32),
            pltpu.VMEM((1024, 128), F32),
        ],
        compiler_params=pltpu.CompilerParams(vmem_limit_bytes=60 << 20),
        cost_estimate=pl.CostEstimate(
            flops=10 * 2048 * 3712 * 128, bytes_accessed=10 << 20, transcendentals=2048 * 3712
        ),
        name="attention",
    )(place, *qg, own, other, far, far_other)
    oq = outs[0:4]
    d_own, d_resp, d_other, d_far, d_far_other = outs[4:9]

    got_far = to_core(d_far_other)
    got_other = to_core(d_other)
    oq = spread(oq, -1)
    there = (d_far + got_far.astype(F32)).astype(BF)
    here = to_pair(there)
    dr = small(sum_resp, "sum_resp", [shape((256, 128))] * 4, 2, False)(d_resp, got_other)
    dr = spread(dr, -1)
    dp = small(sum_prompt, "sum_prompt", [shape((384, 128))] * 4, 3, False)(d_own, got_other, here)
    dp = spread(dp, -1)
    attn_out, query_grad = small(unpack_rows, "unpack_rows", [shape((128, 2048))] * 2, 4)(
        place, *oq
    )
    pk, pv, rk, rv = small(
        unpack_keys, "unpack_keys", [shape((192, 512))] * 2 + [shape((128, 512))] * 2, 8
    )(place, *dp, *dr)
    return attn_out[None], query_grad[None], rk[None], rv[None], pk, pv


def solution(mesh):
    placed = (
        P(("batch", "pair", "ctx"), None),
        P(("batch", "pair", "ctx"), None),
        P("pair", ("batch", "ctx"), None),
        P("pair", ("batch", "ctx"), None),
        P("pair", ("batch", "ctx"), None),
        P("pair", ("batch", "ctx"), None),
        P(("batch", "pair")),
    )
    return jax.shard_map(
        per_device,
        mesh=mesh,
        in_specs=placed,
        out_specs=(
            P("pair", ("batch", "ctx"), None),
            P("pair", ("batch", "ctx"), None),
            P("pair", ("batch", "ctx"), None),
            P("pair", ("batch", "ctx"), None),
            P(("batch", "pair", "ctx"), None),
            P(("batch", "pair", "ctx"), None),
        ),
        check_vma=False,
    )
```
